256 devices in a mesh: seq: 32 (over x, z_hi, core), basis: 8 (over z_lo, y).
Axes of the slice: x: 4, y: 4, z: 8 (z_hi: 4, z_lo: 2; z = z_hi * 2 + z_lo), core: 2. Of those that a mesh axis runs over, the one named last changes fastest.
Arguments:
- activations: bfloat16 [192, 128, 4096], P('seq'), may hold values from -6 to 6
- gradients: bfloat16 [192, 128, 4096], P('seq'), may hold values from -6 to 6
- act_basis: bfloat16 [4096, 4096], P('basis', 'seq'), may hold values from -0.09375 to 0.09375
- grad_basis: bfloat16 [4096, 4096], P('basis', 'seq'), may hold values from -0.09375 to 0.09375
Outputs:
- correction: float32 [4096, 4096], P('seq', 'basis')
The draws below stay inside these ranges and needn't reach their ends.
All inputs are finite; a program needn't handle non-finite values.
Results may differ from the reference program's by a relative error of at most 0.00078.
Values may be sent and summed in bfloat16 or wider, within the bound.
No kernel may reach another device: no remote copies, remote signals or barrier semaphores. Data moves between devices by JAX's collectives and lax.ppermute only.
A program may use at most 128 MiB of HBM per device.

```python
import jax
import jax.numpy as jnp
from jax import lax

D = 4096
LEN = 128
SEQS = 192


def levels(key, shape, split, low, high):
    def one(dim, blocks):
        steps = jax.random.uniform(jax.random.fold_in(jax.random.fold_in(key, 6), dim), (blocks,), jnp.float32, low / len(split), high / len(split))
        return jnp.repeat(jnp.exp(steps), shape[dim] // blocks).reshape((-1,) + (1,) * (len(shape) - dim - 1))

    factor_of = one(*split[0])
    for cut in split[1:]:
        factor_of = factor_of * one(*cut)
    return factor_of


def bell_draw(key, shape, deviation, bound, shards=(), held_as=jnp.bfloat16):
    values = jax.random.normal(key, shape, jnp.float32) * deviation
    if len(shards) > 0:
        values = levels(key, shape, shards, -0.22, 0.18) * values
    return jnp.clip(values, min=-bound, max=bound).astype(held_as)


def setup_inputs(seed: int = 0) -> dict:
    key_of = jax.random.split(jax.random.key(seed), 5)
    return {
        "activations": bell_draw(key_of[0], (SEQS, LEN, D), 1.0, 6.0, ((0, 32),)),
        "gradients": bell_draw(key_of[1], (SEQS, LEN, D), 1.0, 6.0, ((0, 32),)),
        "act_basis": bell_draw(key_of[2], (D, D), D ** -0.5, 0.09375, ((0, 8), (1, 32))),
        "grad_basis": bell_draw(key_of[3], (D, D), D ** -0.5, 0.09375, ((0, 8), (1, 32))),
    }


def rotate(inputs, basis):
    flat_rows = inputs.reshape(-1, inputs.shape[-1]).astype(jnp.float32)
    rotated = jnp.dot(flat_rows, basis.astype(jnp.float32).T)
    return rotated.astype(jnp.bfloat16).reshape(inputs.shape)


def reference(activations, gradients, act_basis, grad_basis):
    rotated_act = rotate(activations, act_basis)
    rotated_grad = rotate(gradients, grad_basis)

    def per_sequence(running, pair):
        left = pair[0].astype(jnp.float32)
        right = pair[1].astype(jnp.float32)
        product = jnp.dot(left.T, right)
        return running + product * product, None

    start_sum = jnp.zeros((D, D), jnp.float32)
    summed, unused = lax.scan(per_sequence, start_sum, (rotated_act, rotated_grad))
    return summed / jnp.float32(SEQS * LEN)
```

```python
import functools

import jax
import jax.numpy as jnp
from jax import lax
from jax.experimental import pallas as pl
from jax.experimental.pallas import tpu as pltpu
from jax.sharding import PartitionSpec as P

NX, NZ, NC, NL, NY = 4, 4, 2, 2, 4
NT = (((1,), (1,)), ((), ()))
VMEM = 48 << 20
BIAS = 14.0


def seq_perm(value, move):
    pairs = []
    for i in range(NX * NZ * NC):
        x, zh, c = move(i // (NZ * NC), i // NC % NZ, i % NC)
        pairs.append((i, ((x % NX) * NZ + zh % NZ) * NC + c % NC))
    return lax.ppermute(value, "seq", pairs)


def basis_perm(value, move):
    pairs = []
    for j in range(NL * NY):
        zl, y = move(j // NY, j % NY)
        pairs.append((j, (zl % NL) * NY + y % NY))
    return lax.ppermute(value, "basis", pairs)


def swap_core(value):
    return seq_perm(value, lambda x, zh, c: (x, zh, c + 1))


def from_x(value, d):
    return seq_perm(value, lambda x, zh, c: (x - d, zh, c))


def from_zh(value, d):
    return seq_perm(value, lambda x, zh, c: (x, zh - d, c))


def from_y(value, d):
    return basis_perm(value, lambda zl, y: (zl, y - d))


def swap_zl(value):
    return basis_perm(value, lambda zl, y: (zl + 1, y))


def to_owner(value):
    pairs = []
    for i in range(NX * NZ * NC):
        for j in range(NL * NY):
            xt, zt, c, zl, y = i // (NZ * NC), i // NC % NZ, i % NC, j // NY, j % NY
            x, zh, core = 2 * ((xt // 2) ^ zl) + y // 2, 2 * (y % 2) + c, xt % 2
            seq, basis = (x * NZ + zh) * NC + core, zl * NY + (y + zt) % NY
            pairs.append((i * NL * NY + j, seq * NL * NY + basis))
    return lax.ppermute(value, ("seq", "basis"), pairs)


def rotate_kernel(flip, tiles, places, own, sibling, p0, p1, p2, p3, out, rows_of):
    step = pl.program_id(0)
    width = p0.shape[2]

    @pl.when(step == 0)
    def _():
        for d, piece in enumerate((p0, p1, p2, p3)):
            for q in range(NZ):
                at = pl.multiple_of(places[d * NZ + q] * width, width)
                rows_of[:, pl.ds(at, width)] = piece[q]

    tile = own.shape[0]
    for half, block in enumerate((own, sibling)):

        @pl.when(step // tiles == half)
        def _():
            total = lax.dot_general(block[...], rows_of[...], NT, preferred_element_type=jnp.float32)
            slot = (places[NX * NZ] ^ half) * tiles + step - half * tiles
            at = pl.multiple_of(slot * tile, tile)
            if flip:
                out[:, pl.ds(at, tile)] = total.T.astype(jnp.bfloat16)
            else:
                out[pl.ds(at, tile), :] = total.astype(jnp.bfloat16)


def rotate(places, own, sibling, pieces, flip):
    tokens, width = own.shape
    rows = pieces[0].shape[1]
    tiles = 3
    shape = (rows, 2 * tokens) if flip else (2 * tokens, rows)
    whole = pl.BlockSpec(pieces[0].shape, lambda s, places: (0, 0, 0))
    return pl.pallas_call(
        functools.partial(rotate_kernel, flip, tiles),
        out_shape=jax.ShapeDtypeStruct(shape, jnp.bfloat16),
        grid_spec=pltpu.PrefetchScalarGridSpec(
            num_scalar_prefetch=1,
            grid=(2 * tiles,),
            in_specs=[
                pl.BlockSpec((tokens // tiles, width), lambda s, places: (jnp.minimum(s, tiles - 1), 0)),
                pl.BlockSpec((tokens // tiles, width), lambda s, places: (jnp.maximum(s - tiles, 0), 0)),
            ]
            + [whole] * 4,
            out_specs=pl.BlockSpec(shape, lambda s, places: (0, 0)),
            scratch_shapes=[pltpu.VMEM((rows, width), jnp.bfloat16)],
        ),
        compiler_params=pltpu.CompilerParams(vmem_limit_bytes=VMEM),
        cost_estimate=pl.CostEstimate(
            flops=4 * tokens * rows * width, bytes_accessed=4 * tokens * width, transcendentals=0
        ),
    )(places, own, sibling, *pieces)


def product_kernel(seq_len, places, left0, left1, *rest):
    grads, out, left = rest[:8], rest[8], rest[9]
    step = pl.program_id(0)
    half = left0.shape[0]
    rows = 2 * half // NX
    width = grads[0].shape[1]

    @pl.when(step == 0)
    def _():
        left[:half, :] = left0[...]
        left[half:, :] = left1[...]

    piece = left[pl.ds(pl.multiple_of(places[step] * rows, rows), rows), :]
    top = jnp.zeros((1, 1), jnp.float32)
    for g in range(8):
        total = None
        for s in range(piece.shape[1] // seq_len):
            tokens = slice(s * seq_len, (s + 1) * seq_len)
            product = jnp.dot(piece[:, tokens], grads[g][tokens, :], preferred_element_type=jnp.float32)
            total = product * product if total is None else total + product * product
        row = pl.multiple_of(places[4 + g // 2] * rows, rows)
        column = pl.multiple_of((places[8] ^ (g % 2)) * width, width)
        out[0, pl.ds(row, rows), pl.ds(column, width)] = total
        top = jnp.maximum(top, jnp.max(jnp.max(total, axis=0, keepdims=True), axis=1, keepdims=True))
    power = jnp.clip(jnp.ceil(jnp.log2(top)), -100.0, 130.0)
    out[0, 4 * rows :, :] = jnp.broadcast_to(power, (16, 2 * width))


def products(places, left, grads, seq_len):
    half, tokens = left[0].shape
    width = grads[0].shape[1]
    shape = (NX, 2 * half + 16, 2 * width)
    return pl.pallas_call(
        functools.partial(product_kernel, seq_len),
        out_shape=jax.ShapeDtypeStruct(shape, jnp.float32),
        grid_spec=pltpu.PrefetchScalarGridSpec(
            num_scalar_prefetch=1,
            grid=(NX,),
            in_specs=[pl.BlockSpec((half, tokens), lambda s, places: (0, 0))] * 2
            + [pl.BlockSpec((tokens, width), lambda s, places: (0, 0))] * 8,
            out_specs=pl.BlockSpec((1,) + shape[1:], lambda s, places: (s, 0, 0)),
            scratch_shapes=[pltpu.VMEM((2 * half, tokens), jnp.bfloat16)],
        ),
        compiler_params=pltpu.CompilerParams(vmem_limit_bytes=VMEM),
        cost_estimate=pl.CostEstimate(
            flops=16 * half * tokens * width, bytes_accessed=20 * tokens * width, transcendentals=0
        ),
    )(places, *left, *grads)


def shrink(block, power):
    return block * jnp.exp2(BIAS - power)


def grow(sent):
    power = sent[-1, 0].astype(jnp.float32)
    return sent[:-16].astype(jnp.float32) * jnp.exp2(power - BIAS)


def gather_rows(shard):
    column = jnp.stack([shard] + [from_zh(shard, d) for d in range(1, NZ)])
    return [column] + [from_x(column, d) for d in range(1, NX)]


def per_device(activations, gradients, act_basis, grad_basis):
    seq_count, seq_len, width = activations.shape
    seq, basis = lax.axis_index("seq"), lax.axis_index("basis")
    x, zh, core = seq // (NZ * NC), seq // NC % NZ, seq % NC
    act = activations.reshape(seq_count * seq_len, width)
    grad = gradients.reshape(seq_count * seq_len, width)

    half = act_basis.shape[0] // 2

    def mine(shard, which):
        return lax.dynamic_slice_in_dim(shard, which * half, half, 0)

    kept = jnp.concatenate([mine(grad_basis, core), mine(act_basis, core)])
    got = swap_core(jnp.concatenate([mine(grad_basis, 1 - core), mine(act_basis, 1 - core)]))
    pair = jnp.where(core == 0, jnp.concatenate([kept, got], 1), jnp.concatenate([got, kept], 1))
    grad_pieces = gather_rows(pair[:half])
    act_pieces = gather_rows(pair[half:])
    grad_sib, act_sib = swap_core(grad), swap_core(act)

    steps = jnp.arange(4)
    feature_of = ((x + steps[:, None]) % NX) * NZ + (zh + steps[None, :]) % NZ
    places = jnp.concatenate([feature_of.reshape(-1), core[None]]).astype(jnp.int32)
    rotated_grad = rotate(places, grad, grad_sib, grad_pieces, False)
    rotated_act = rotate(places, act, act_sib, act_pieces, True)

    grads = [rotated_grad] + [from_y(rotated_grad, d) for d in range(1, NY)]
    both = []
    for block in grads:
        both += [block, swap_core(block)]
    left = [rotated_act, swap_zl(rotated_act)]

    places = jnp.concatenate([(x + steps) % NX, (steps - zh) % NZ, core[None]]).astype(jnp.int32)
    terms = products(places, left, both, seq_len)

    def packed(d):
        term = terms[d]
        power = term[-1, 0]
        inside = lax.broadcasted_iota(jnp.int32, term.shape, 0) < term.shape[0] - 16
        return jnp.where(inside, shrink(term, power), power).astype(jnp.float16)

    total = terms[0, :-16]
    for d in range(1, NX):
        total = total + grow(from_x(packed(d), -d))
    rows = total.shape[0] // NZ
    power = jnp.clip(jnp.ceil(jnp.log2(jnp.max(total))), -100.0, 130.0)
    final = total[:rows]
    for d in range(1, NZ):
        block = shrink(total[d * rows : (d + 1) * rows], power)
        sent = jnp.concatenate([block, jnp.full((16, block.shape[1]), power)]).astype(jnp.float16)
        final = final + grow(from_zh(sent, -d))
    all_seqs = seq_count * NX * NZ * NC
    return to_owner(final / jnp.float32(all_seqs * seq_len))


def solution(mesh):
    placed = (P("seq", None, None), P("seq", None, None), P("basis", "seq"), P("basis", "seq"))
    return jax.shard_map(
        per_device, mesh=mesh, in_specs=placed, out_specs=P("seq", "basis"), check_vma=False
    )
```

```python
import functools

import jax
import jax.numpy as jnp
from jax import lax
from jax.experimental import pallas as pl
from jax.experimental.pallas import tpu as pltpu
from jax.sharding import PartitionSpec as P

NX, NZ, NC, NL, NY = 4, 4, 2, 2, 4
VMEM = 26 << 20
BIAS = 14.0
PAD = 16


def seq_perm(value, move):
    pairs = []
    for i in range(NX * NZ * NC):
        x, zh, c = move(i // (NZ * NC), i // NC % NZ, i % NC)
        pairs.append((i, ((x % NX) * NZ + zh % NZ) * NC + c % NC))
    return lax.ppermute(value, "seq", pairs)


def basis_perm(value, move):
    pairs = []
    for j in range(NL * NY):
        zl, y = move(j // NY, j % NY)
        pairs.append((j, (zl % NL) * NY + y % NY))
    return lax.ppermute(value, "basis", pairs)


def swap_core(value):
    return seq_perm(value, lambda x, zh, c: (x, zh, c + 1))


def from_x(value, d):
    return seq_perm(value, lambda x, zh, c: (x - d, zh, c))


def from_zh(value, d):
    return seq_perm(value, lambda x, zh, c: (x, zh - d, c))


def from_y(value, d):
    return basis_perm(value, lambda zl, y: (zl, y - d))


def swap_zl(value):
    return basis_perm(value, lambda zl, y: (zl + 1, y))


def all_x(copies):
    groups = [[(x * NZ + zh) * NC + c for x in range(NX)] for zh in range(NZ) for c in range(NC)]
    return lax.all_to_all(copies, "seq", 0, 0, axis_index_groups=groups, tiled=True)


def to_owner(value, k):
    pairs = []
    for i in range(NX * NZ * NC):
        for j in range(NL * NY):
            xt, zt, c, zl, y = i // (NZ * NC), i // NC % NZ, i % NC, j // NY, j % NY
            x, zh, core = xt - xt % 2 + y // 2, 2 * (y % 2) + c, (xt % 2) ^ (y // 2)
            seq, basis = (x * NZ + zh) * NC + core, zl * NY + (y + zt + k) % NY
            pairs.append((i * NL * NY + j, seq * NL * NY + basis))
    return lax.ppermute(value, ("seq", "basis"), pairs)


def power_of(top):
    return jnp.clip(jnp.ceil(jnp.log2(top)), -100.0, 130.0)


def grow(sent):
    wide = sent.astype(jnp.float32)
    return wide[:-PAD] * jnp.exp2(wide[-PAD : 1 - PAD] - BIAS)


def product_kernel(seq_len, places, left0, left1, left2, *rest):
    grads, (out, left, right, left_sem, right_sem) = rest[:8], rest[8:]
    rows = left1.shape[0]
    width = grads[0].shape[1]
    seqs = left.shape[1] // seq_len
    lefts = [
        pltpu.make_async_copy(ref, left.at[pl.ds(at * rows, ref.shape[0]), :], left_sem.at[i])
        for i, (at, ref) in enumerate(((0, left0), (2, left1), (3, left2)))
    ]
    rights = [pltpu.make_async_copy(ref, right.at[g], right_sem.at[g]) for g, ref in enumerate(grads)]
    for copy in lefts + rights:
        copy.start()
    for copy in lefts:
        copy.wait()

    top = jnp.zeros((8, width), jnp.float32)
    for g in range(8):
        rights[g].wait()
        row = pl.multiple_of(places[NX + g // 2] * rows, rows)
        column = pl.multiple_of((places[NX + NZ] ^ (g % 2)) * width, width)
        shift = seqs // 2 if g % 2 else 0

        def one(d, top):
            at = pl.multiple_of(places[d] * rows, rows)
            total = None
            for s in range(seqs):
                from_token = (s + shift) % seqs * seq_len
                product = jnp.dot(
                    left[pl.ds(at, rows), s * seq_len : (s + 1) * seq_len],
                    right[g, from_token : from_token + seq_len, :],
                    preferred_element_type=jnp.float32,
                )
                total = product * product if total is None else total + product * product
            out[d, pl.ds(row, rows), pl.ds(column, width)] = total
            return jnp.maximum(top, jnp.max(total.reshape(rows // 8, 8, width), axis=0))

        for d in range(NX):
            top = one(d, top)
    power = power_of(jnp.max(jnp.max(top, axis=0, keepdims=True), axis=1, keepdims=True))
    for d in range(1, NX):
        out[d, : NZ * rows, :] = out[d, : NZ * rows, :] * jnp.exp2(BIAS - power)
        out[d, NZ * rows :, :] = jnp.broadcast_to(power, (PAD, 2 * width))
    out[0, NZ * rows :, :] = jnp.full((PAD, 2 * width), BIAS)


def products(places, left, grads, seq_len):
    half, tokens = left[0].shape
    width = grads[0].shape[1]
    return pl.pallas_call(
        functools.partial(product_kernel, seq_len),
        out_shape=jax.ShapeDtypeStruct((NX, 2 * half + PAD, 2 * width), jnp.float32),
        in_specs=[pl.BlockSpec(memory_space=pltpu.SMEM)] + [pl.BlockSpec(memory_space=pl.ANY)] * 11,
        out_specs=pl.BlockSpec(memory_space=pltpu.VMEM),
        scratch_shapes=[
            pltpu.VMEM((2 * half, tokens), jnp.bfloat16),
            pltpu.VMEM((8, tokens, width), jnp.bfloat16),
            pltpu.SemaphoreType.DMA((3,)),
            pltpu.SemaphoreType.DMA((8,)),
        ],
        compiler_params=pltpu.CompilerParams(vmem_limit_bytes=VMEM),
        cost_estimate=pl.CostEstimate(
            flops=32 * half * tokens * width, bytes_accessed=20 * tokens * width, transcendentals=0
        ),
    )(places, *left, *grads)


def stack_zh(shard, zh):
    column = jnp.stack([shard] + [from_zh(shard, d) for d in range(1, NZ)])
    twice = jnp.concatenate([column, column])
    column = lax.dynamic_slice_in_dim(twice, (NZ - zh) % NZ, NZ, 0)
    return column.reshape(NZ * shard.shape[0], shard.shape[1])


def per_device(activations, gradients, act_basis, grad_basis):
    seq_count, seq_len, width = activations.shape
    seq, basis = lax.axis_index("seq"), lax.axis_index("basis")
    x, zh, core = seq // (NZ * NC), seq // NC % NZ, seq % NC
    zl, y = basis // NY, basis % NY
    act = activations.reshape(seq_count * seq_len, width)
    grad = gradients.reshape(seq_count * seq_len, width)

    half = act_basis.shape[0] // 2

    def rows_at(which):
        start = which * half
        return [lax.dynamic_slice_in_dim(shard, start, half, 0).T for shard in (grad_basis, act_basis)]

    kept = jnp.concatenate(rows_at(core), 1)
    got = swap_core(jnp.concatenate(rows_at(1 - core), 1))
    pair = jnp.where(core == 0, jnp.concatenate([kept, got]), jnp.concatenate([got, kept]))
    grad_column = stack_zh(pair[:, :half], zh)
    copies = jnp.broadcast_to(grad_column[None], (NX,) + grad_column.shape)
    act_pair, copies, grad, act = lax.optimization_barrier((pair[:, half:], copies, grad, act))
    grad_rows = all_x(copies).reshape(-1, half)
    grad_sib = swap_core(grad)
    act_column = stack_zh(act_pair, zh)
    act_sib = swap_core(act)
    act_column, grad_rows, grad_sib, act_sib = lax.optimization_barrier(
        (act_column, grad_rows, grad_sib, act_sib)
    )
    act_columns = [act_column] + [from_x(act_column, d) for d in range(1, NX)]

    def rotate_grad(block):
        return jnp.dot(block, grad_rows, preferred_element_type=jnp.float32).astype(jnp.bfloat16)

    rotated_grad = jnp.concatenate([rotate_grad(grad), rotate_grad(grad_sib)])
    act_columns, fenced = lax.optimization_barrier((act_columns, rotated_grad))
    act_rows = jnp.zeros((NX,) + act_column.shape, act_column.dtype)
    for d in range(NX):
        act_rows = lax.dynamic_update_slice(act_rows, act_columns[d][None], ((x + d) % NX, 0, 0))
    act_rows = act_rows.reshape(-1, half)

    def rotate_act(block):
        total = lax.dot_general(
            act_rows, block, (((0,), (1,)), ((), ())), preferred_element_type=jnp.float32
        )
        return total.astype(jnp.bfloat16)

    rotated_act = jnp.concatenate([rotate_act(act), rotate_act(act_sib)], 1)

    far = [from_y(rotated_grad, d) for d in range(1, NY)]
    pieces = [swap_zl(rotated_act[: half // 2]), swap_zl(rotated_act[half // 2 :])]
    far, near, pieces = lax.optimization_barrier((far, rotated_act, pieces))
    both = []
    for block in [fenced] + far:
        both += [block, swap_core(block)]

    steps = jnp.arange(4)
    target = (x + steps) % NX
    rows_of = 2 * ((target // 2) ^ zl) + ((target % 2) ^ (y // 2))
    places = jnp.concatenate([rows_of, (steps - zh) % NZ, core[None]]).astype(jnp.int32)
    terms = products(places, [near] + pieces, both, seq_len)

    total = terms[0, :-PAD]
    for d in range(1, NX):
        total = total + grow(from_x(terms[d].astype(jnp.float16), -d))
    rows = total.shape[0] // NZ
    power = power_of(jnp.max(total))
    final = None
    for k in range(NZ):
        block = total[k * rows : (k + 1) * rows] * jnp.exp2(BIAS - power)
        sent = jnp.concatenate([block, jnp.full((PAD, block.shape[1]), power)]).astype(jnp.float16)
        part = grow(to_owner(sent, k))
        final = part if final is None else final + part
    all_seqs = seq_count * NX * NZ * NC
    return final / jnp.float32(all_seqs * seq_len)


def solution(mesh):
    placed = (P("seq", None, None), P("seq", None, None), P("basis", "seq"), P("basis", "seq"))
    return jax.shard_map(
        per_device, mesh=mesh, in_specs=placed, out_specs=P("seq", "basis"), check_vma=False
    )
```

```python
import functools

import jax
import jax.numpy as jnp
from jax import lax
from jax.experimental import pallas as pl
from jax.experimental.pallas import tpu as pltpu
from jax.sharding import PartitionSpec as P

NX, NZ, NC, NL, NY = 4, 4, 2, 2, 4
VMEM = 16 << 20
BIAS = 14.0
PAD = 16


def seq_perm(value, move):
    pairs = []
    for i in range(NX * NZ * NC):
        x, zh, c = move(i // (NZ * NC), i // NC % NZ, i % NC)
        pairs.append((i, ((x % NX) * NZ + zh % NZ) * NC + c % NC))
    return lax.ppermute(value, "seq", pairs)


def basis_perm(value, move):
    pairs = []
    for j in range(NL * NY):
        zl, y = move(j // NY, j % NY)
        pairs.append((j, (zl % NL) * NY + y % NY))
    return lax.ppermute(value, "basis", pairs)


def swap_core(value):
    return seq_perm(value, lambda x, zh, c: (x, zh, c + 1))


def from_x(value, d):
    return seq_perm(value, lambda x, zh, c: (x - d, zh, c))


def from_zh(value, d):
    return seq_perm(value, lambda x, zh, c: (x, zh - d, c))


def from_y(value, d):
    return basis_perm(value, lambda zl, y: (zl, y - d))


def swap_zl(value):
    return basis_perm(value, lambda zl, y: (zl + 1, y))


def to_owner(value, k):
    pairs = []
    for i in range(NX * NZ * NC):
        for j in range(NL * NY):
            xt, zt, c, zl, y = i // (NZ * NC), i // NC % NZ, i % NC, j // NY, j % NY
            x, zh, core = xt - xt % 2 + y // 2, 2 * (y % 2) + c, (xt % 2) ^ (y // 2)
            seq, basis = (x * NZ + zh) * NC + core, zl * NY + (y + zt + k) % NY
            pairs.append((i * NL * NY + j, seq * NL * NY + basis))
    return lax.ppermute(value, ("seq", "basis"), pairs)


def power_of(top):
    return jnp.clip(jnp.ceil(jnp.log2(top)), -100.0, 130.0)


def grow(sent):
    wide = sent.astype(jnp.float32)
    return wide[:-PAD] * jnp.exp2(wide[-PAD : 1 - PAD] - BIAS)


def product_kernel(seq_len, turn, places, left0, left1, left2, *rest):
    grads, (out, left, right, left_sem, right_sem) = rest[:NY], rest[NY:]
    rows = left1.shape[0]
    width = grads[0].shape[1]
    seqs = left.shape[1] // seq_len
    lefts = [
        pltpu.make_async_copy(ref, left.at[pl.ds(at * rows, ref.shape[0]), :], left_sem.at[i])
        for i, (at, ref) in enumerate(((0, left0), (2, left1), (3, left2)))
    ]
    rights = [pltpu.make_async_copy(ref, right.at[g], right_sem.at[g]) for g, ref in enumerate(grads)]
    for copy in lefts + rights:
        copy.start()
    for copy in lefts:
        copy.wait()

    top = jnp.zeros((8, width), jnp.float32)
    for g in range(NY):
        rights[g].wait()

        def one(d, top):
            at = pl.multiple_of(places[d] * rows, rows)
            total = None
            for s in range(seqs):
                from_token = (s + turn) % seqs * seq_len
                product = jnp.dot(
                    left[pl.ds(at, rows), s * seq_len : (s + 1) * seq_len],
                    right[g, from_token : from_token + seq_len, :],
                    preferred_element_type=jnp.float32,
                )
                total = product * product if total is None else total + product * product
            out[d, g * rows : (g + 1) * rows, :] = total
            return jnp.maximum(top, jnp.max(total.reshape(rows // 8, 8, width), axis=0))

        for d in range(NX):
            top = one(d, top)
    power = power_of(jnp.max(jnp.max(top, axis=0, keepdims=True), axis=1, keepdims=True))
    for d in range(NX):
        out[d, : NY * rows, :] = out[d, : NY * rows, :] * jnp.exp2(BIAS - power)
        out[d, NY * rows :, :] = jnp.broadcast_to(power, (PAD, width))


def products(places, left, grads, seq_len, turn):
    half, tokens = left[0].shape
    width = grads[0].shape[1]
    return pl.pallas_call(
        functools.partial(product_kernel, seq_len, turn),
        out_shape=jax.ShapeDtypeStruct((NX, 2 * half + PAD, width), jnp.float32),
        in_specs=[pl.BlockSpec(memory_space=pltpu.SMEM)] + [pl.BlockSpec(memory_space=pl.ANY)] * 7,
        out_specs=pl.BlockSpec(memory_space=pltpu.VMEM),
        scratch_shapes=[
            pltpu.VMEM((2 * half, tokens), jnp.bfloat16),
            pltpu.VMEM((NY, tokens, width), jnp.bfloat16),
            pltpu.SemaphoreType.DMA((3,)),
            pltpu.SemaphoreType.DMA((NY,)),
        ],
        compiler_params=pltpu.CompilerParams(vmem_limit_bytes=VMEM),
        cost_estimate=pl.CostEstimate(
            flops=16 * half * tokens * width, bytes_accessed=10 * tokens * width, transcendentals=0
        ),
    )(places, *left, *grads)


def settle_kernel(value, out, sem):
    copy = pltpu.make_async_copy(value, out, sem)
    copy.start()
    copy.wait()


def settle(value):
    return pl.pallas_call(
        settle_kernel,
        out_shape=jax.ShapeDtypeStruct(value.shape, value.dtype),
        in_specs=[pl.BlockSpec(memory_space=pl.ANY)],
        out_specs=pl.BlockSpec(memory_space=pltpu.VMEM),
        scratch_shapes=[pltpu.SemaphoreType.DMA],
        compiler_params=pltpu.CompilerParams(vmem_limit_bytes=VMEM),
    )(value)


def in_order(pieces, zh):
    twice = jnp.stack(pieces + pieces)
    column = lax.dynamic_slice_in_dim(twice, (NZ - zh) % NZ, NZ, 0)
    return column.reshape(-1, column.shape[2])


def per_device(activations, gradients, act_basis, grad_basis):
    seq_count, seq_len, width = activations.shape
    seq, basis = lax.axis_index("seq"), lax.axis_index("basis")
    x, zh, core = seq // (NZ * NC), seq // NC % NZ, seq % NC
    zl, y = basis // NY, basis % NY
    act = activations.reshape(seq_count * seq_len, width)
    grad = gradients.reshape(seq_count * seq_len, width)

    half = act_basis.shape[0] // 2

    def rows_at(which):
        start = which * half
        return [lax.dynamic_slice_in_dim(shard, start, half, 0).T for shard in (grad_basis, act_basis)]

    kept = jnp.stack(rows_at(core))
    got = swap_core(jnp.stack(rows_at(1 - core)))
    pair = jnp.where(core == 0, jnp.concatenate([kept, got], 1), jnp.concatenate([got, kept], 1))
    pair, grad, act = lax.optimization_barrier((pair, grad, act))
    pieces = [pair] + [from_zh(pair, d) for d in range(1, NZ)]
    grad_sib, act_sib = settle(swap_core(grad)), settle(swap_core(act))
    pieces, grad_sib, act_sib = lax.optimization_barrier((pieces, grad_sib, act_sib))
    grad_column = in_order([piece[0] for piece in pieces], zh)
    act_column = in_order([piece[1] for piece in pieces], zh)
    grad_columns = [grad_column] + [from_x(grad_column, d) for d in range(1, NX)]
    depth = grad_column.shape[0]

    def term(block, columns, d, dims):
        part = lax.dynamic_slice_in_dim(block, (x + d) % NX * depth, depth, 1)
        sides = (part, columns[d]) if dims[0] == 1 else (columns[d], part)
        return lax.dot_general(*sides, ((dims[:1], dims[1:]), ((), ())), preferred_element_type=jnp.float32)

    def begin(blocks, columns, dims):
        sums = [term(block, columns, 0, dims) for block in blocks]
        later, sums = lax.optimization_barrier((columns[2:], sums))
        columns = columns[:2] + later
        return [
            total + term(block, columns, 3, dims) + term(block, columns, 2, dims)
            for block, total in zip(blocks, sums)
        ]

    def end(blocks, columns, dims, sums):
        totals = [total + term(block, columns, 1, dims) for block, total in zip(blocks, sums)]
        return jnp.concatenate([total.astype(jnp.bfloat16) for total in totals], dims[1])

    blocks = [grad, grad_sib]
    sums = begin(blocks, grad_columns, (1, 0))
    grad_columns, act_column, act_sib, sums = lax.optimization_barrier(
        (grad_columns, act_column, act_sib, sums)
    )
    act_columns = [act_column] + [from_x(act_column, d) for d in range(1, NX)]
    rotated_grad = end(blocks, grad_columns, (1, 0), sums)
    blocks = [act, act_sib]
    sums = begin(blocks, act_columns, (0, 1))
    act_columns, fenced, sums = lax.optimization_barrier((act_columns, rotated_grad, sums))
    rotated_act = end(blocks, act_columns, (0, 1), sums)

    far = [from_y(rotated_grad, d) for d in range(1, NY)]
    pieces = [swap_zl(rotated_act[: half // 2]), swap_zl(rotated_act[half // 2 :])]
    far, near, pieces = lax.optimization_barrier((far, rotated_act, pieces))
    mine = [fenced] + far
    other = [swap_core(block) for block in mine]

    target = (x + jnp.arange(NX)) % NX
    places = (2 * ((target // 2) ^ zl) + ((target % 2) ^ (y // 2))).astype(jnp.int32)
    left = [near] + pieces
    terms = [
        products(places, left, mine, seq_len, 0),
        products(places, left, other, seq_len, seq_count),
    ]
    received = [[from_x(term[d].astype(jnp.float16), -d) for d in range(1, NX)] for term in terms]
    received = lax.optimization_barrier(received)
    halves = []
    for kept, parts in zip(terms, received):
        half = grow(kept[0])
        for part in parts:
            half = half + grow(part)
        halves.append(half)
    total = jnp.where(core == 0, jnp.concatenate(halves, 1), jnp.concatenate(halves[::-1], 1))
    rows = total.shape[0] // NZ
    power = power_of(jnp.max(total))
    final = None
    for k in range(NZ):
        block = lax.dynamic_slice_in_dim(total, (zh + k) % NZ * rows, rows, 0) * jnp.exp2(BIAS - power)
        sent = jnp.concatenate([block, jnp.full((PAD, block.shape[1]), power)]).astype(jnp.float16)
        part = grow(to_owner(sent, k))
        final = part if final is None else final + part
    all_seqs = seq_count * NX * NZ * NC
    return final / jnp.float32(all_seqs * seq_len)


def solution(mesh):
    placed = (P("seq", None, None), P("seq", None, None), P("basis", "seq"), P("basis", "seq"))
    return jax.shard_map(
        per_device, mesh=mesh, in_specs=placed, out_specs=P("seq", "basis"), check_vma=False
    )
```

```python
import functools

import jax
import jax.numpy as jnp
from jax import lax
from jax.experimental import pallas as pl
from jax.experimental.pallas import tpu as pltpu
from jax.sharding import PartitionSpec as P

NX, NZ, NC, NL, NY = 4, 4, 2, 2, 4
VMEM = 16 << 20
BIAS = 14.0
PAD = 16


def seq_perm(value, move):
    pairs = []
    for i in range(NX * NZ * NC):
        x, zh, c = move(i // (NZ * NC), i // NC % NZ, i % NC)
        pairs.append((i, ((x % NX) * NZ + zh % NZ) * NC + c % NC))
    return lax.ppermute(value, "seq", pairs)


def basis_perm(value, move):
    pairs = []
    for j in range(NL * NY):
        zl, y = move(j // NY, j % NY)
        pairs.append((j, (zl % NL) * NY + y % NY))
    return lax.ppermute(value, "basis", pairs)


def swap_core(value):
    return seq_perm(value, lambda x, zh, c: (x, zh, c + 1))


def from_x(value, d):
    return seq_perm(value, lambda x, zh, c: (x - d, zh, c))


def from_zh(value, d):
    return seq_perm(value, lambda x, zh, c: (x, zh - d, c))


def from_y(value, d):
    return basis_perm(value, lambda zl, y: (zl, y - d))


def swap_zl(value):
    return basis_perm(value, lambda zl, y: (zl + 1, y))


def to_owner(value, k):
    pairs = []
    for i in range(NX * NZ * NC):
        for j in range(NL * NY):
            xt, zt, c, zl, y = i // (NZ * NC), i // NC % NZ, i % NC, j // NY, j % NY
            x, zh, ahead = xt - xt % 2 + y // 2, 2 * (y % 2) + c, 2 * ((xt % 2) ^ (y // 2)) + (zt + k) % 2
            seq, basis = (x * NZ + zh) * NC + zt // 2, zl * NY + (y + ahead) % NY
            pairs.append((i * NL * NY + j, seq * NL * NY + basis))
    return lax.ppermute(value, ("seq", "basis"), pairs)


def power_of(top):
    return jnp.clip(jnp.ceil(jnp.log2(top)), -100.0, 130.0)


def grow(sent):
    wide = sent.astype(jnp.float32)
    return wide[:-PAD] * jnp.exp2(wide[-PAD : 1 - PAD] - BIAS)


def product_kernel(seq_len, turn, places, left0, left1, left2, *rest):
    grads, (out, left, right, left_sem, right_sem) = rest[:NY], rest[NY:]
    rows = left1.shape[0]
    width = grads[0].shape[1]
    seqs = left.shape[1] // seq_len
    lefts = [
        pltpu.make_async_copy(ref, left.at[pl.ds(at * rows, ref.shape[0]), :], left_sem.at[i])
        for i, (at, ref) in enumerate(((0, left0), (2, left1), (3, left2)))
    ]
    rights = [pltpu.make_async_copy(ref, right.at[g], right_sem.at[g]) for g, ref in enumerate(grads)]
    for copy in lefts + rights:
        copy.start()
    for copy in lefts:
        copy.wait()

    top = jnp.zeros((8, width), jnp.float32)
    for g in range(NY):
        rights[g].wait()

        for m in range(4):
            total = None
            for s in range(seqs):
                from_token = (s + turn) % seqs * seq_len
                product = jnp.dot(
                    left[m * rows : (m + 1) * rows, s * seq_len : (s + 1) * seq_len],
                    right[g, from_token : from_token + seq_len, :],
                    preferred_element_type=jnp.float32,
                )
                total = product * product if total is None else total + product * product
            row = (g % 2 * 2 + m % 2) * rows
            out[places[m // 2 * 2 + g // 2], row : row + rows, :] = total
            top = jnp.maximum(top, jnp.max(total.reshape(rows // 8, 8, width), axis=0))
    power = power_of(jnp.max(jnp.max(top, axis=0, keepdims=True), axis=1, keepdims=True))
    for d in range(NX):
        out[d, : NY * rows, :] = out[d, : NY * rows, :] * jnp.exp2(BIAS - power)
        out[d, NY * rows :, :] = jnp.broadcast_to(power, (PAD, width))


def products(places, left, grads, seq_len, turn):
    half, tokens = left[0].shape
    width = grads[0].shape[1]
    return pl.pallas_call(
        functools.partial(product_kernel, seq_len, turn),
        out_shape=jax.ShapeDtypeStruct((NX, 2 * half + PAD, width), jnp.float32),
        in_specs=[pl.BlockSpec(memory_space=pltpu.SMEM)] + [pl.BlockSpec(memory_space=pl.ANY)] * 7,
        out_specs=pl.BlockSpec(memory_space=pltpu.VMEM),
        scratch_shapes=[
            pltpu.VMEM((2 * half, tokens), jnp.bfloat16),
            pltpu.VMEM((NY, tokens, width), jnp.bfloat16),
            pltpu.SemaphoreType.DMA((3,)),
            pltpu.SemaphoreType.DMA((NY,)),
        ],
        compiler_params=pltpu.CompilerParams(vmem_limit_bytes=VMEM),
        cost_estimate=pl.CostEstimate(
            flops=16 * half * tokens * width, bytes_accessed=10 * tokens * width, transcendentals=0
        ),
    )(places, *left, *grads)


def settle_kernel(value, out, sem):
    copy = pltpu.make_async_copy(value, out, sem)
    copy.start()
    copy.wait()


def settle(value):
    return pl.pallas_call(
        settle_kernel,
        out_shape=jax.ShapeDtypeStruct(value.shape, value.dtype),
        in_specs=[pl.BlockSpec(memory_space=pl.ANY)],
        out_specs=pl.BlockSpec(memory_space=pltpu.VMEM),
        scratch_shapes=[pltpu.SemaphoreType.DMA],
        compiler_params=pltpu.CompilerParams(vmem_limit_bytes=VMEM),
    )(value)


def in_order(pieces, zh):
    twice = jnp.stack(pieces + pieces)
    column = lax.dynamic_slice_in_dim(twice, (NZ - zh) % NZ, NZ, 0)
    return column.reshape(-1, column.shape[2])


def per_device(activations, gradients, act_basis, grad_basis):
    seq_count, seq_len, width = activations.shape
    seq, basis = lax.axis_index("seq"), lax.axis_index("basis")
    x, zh, core = seq // (NZ * NC), seq // NC % NZ, seq % NC
    zl, y = basis // NY, basis % NY
    act = activations.reshape(seq_count * seq_len, width)
    grad = gradients.reshape(seq_count * seq_len, width)

    half = act_basis.shape[0] // 2

    def rows_at(which):
        start = which * half
        return [lax.dynamic_slice_in_dim(shard, start, half, 0).T for shard in (grad_basis, act_basis)]

    kept = jnp.stack(rows_at(core))
    got = swap_core(jnp.stack(rows_at(1 - core)))
    pair = jnp.where(core == 0, jnp.concatenate([kept, got], 1), jnp.concatenate([got, kept], 1))
    pair, grad, act = lax.optimization_barrier((pair, grad, act))
    pieces = [pair] + [from_zh(pair, d) for d in range(1, NZ)]
    grad_sib, act_sib = settle(swap_core(grad)), settle(swap_core(act))
    pieces, grad_sib, act_sib = lax.optimization_barrier((pieces, grad_sib, act_sib))
    grad_column = in_order([piece[0] for piece in pieces], zh)
    act_column = in_order([piece[1] for piece in pieces], zh)
    grad_columns = [grad_column] + [from_x(grad_column, d) for d in range(1, NX)]
    depth = grad_column.shape[0]

    def term(block, columns, d, dims):
        part = lax.dynamic_slice_in_dim(block, (x + d) % NX * depth, depth, 1)
        sides = (part, columns[d]) if dims[0] == 1 else (columns[d], part)
        return lax.dot_general(*sides, ((dims[:1], dims[1:]), ((), ())), preferred_element_type=jnp.float32)

    def begin(blocks, columns, dims):
        sums = [term(block, columns, 0, dims) for block in blocks]
        later, sums = lax.optimization_barrier((columns[2:], sums))
        columns = columns[:2] + later
        return [
            total + term(block, columns, 3, dims) + term(block, columns, 2, dims)
            for block, total in zip(blocks, sums)
        ]

    def end(blocks, columns, dims, sums):
        totals = [total + term(block, columns, 1, dims) for block, total in zip(blocks, sums)]
        return jnp.concatenate([total.astype(jnp.bfloat16) for total in totals], dims[1])

    blocks = [grad, grad_sib]
    sums = begin(blocks, grad_columns, (1, 0))
    grad_columns, act_column, act_sib, sums = lax.optimization_barrier(
        (grad_columns, act_column, act_sib, sums)
    )
    act_columns = [act_column] + [from_x(act_column, d) for d in range(1, NX)]
    rotated_grad = end(blocks, grad_columns, (1, 0), sums)
    blocks = [act, act_sib]
    sums = begin(blocks, act_columns, (0, 1))
    act_columns, fenced, sums = lax.optimization_barrier((act_columns, rotated_grad, sums))
    rotated_act = end(blocks, act_columns, (0, 1), sums)

    far = [from_y(rotated_grad, d) for d in range(1, NY)]
    pieces = [swap_zl(rotated_act[: half // 2]), swap_zl(rotated_act[half // 2 :])]
    far, near, pieces = lax.optimization_barrier((far, rotated_act, pieces))
    mine = [fenced] + far
    other = [swap_core(block) for block in mine]

    number = jnp.arange(NX)
    target = 2 * ((number // 2) ^ zl) + ((number % 2) ^ (y // 2))
    places = ((target - x) % NX).astype(jnp.int32)
    left = [near] + pieces
    terms = [
        products(places, left, mine, seq_len, 0),
        products(places, left, other, seq_len, seq_count),
    ]
    received = [[from_x(term[d].astype(jnp.float16), -d) for d in range(1, NX)] for term in terms]
    received = lax.optimization_barrier(received)
    halves = []
    for kept, parts in zip(terms, received):
        half = grow(kept[0])
        for part in parts:
            half = half + grow(part)
        halves.append(half)
    total = jnp.where(core == 0, jnp.concatenate(halves, 1), jnp.concatenate(halves[::-1], 1))
    rows = total.shape[0] // 2
    power = power_of(jnp.max(total))
    both = None
    for k in range(2):
        block = lax.dynamic_slice_in_dim(total, (zh + k) % 2 * rows, rows, 0) * jnp.exp2(BIAS - power)
        sent = jnp.concatenate([block, jnp.full((PAD, block.shape[1]), power)]).astype(jnp.float16)
        part = grow(to_owner(sent, k))
        both = part if both is None else both + part
    rows = rows // 2
    final = lax.dynamic_slice_in_dim(both, core * rows, rows, 0)
    final = final + swap_core(lax.dynamic_slice_in_dim(both, (1 - core) * rows, rows, 0))
    all_seqs = seq_count * NX * NZ * NC
    return final / jnp.float32(all_seqs * seq_len)


def solution(mesh):
    placed = (P("seq", None, None), P("seq", None, None), P("basis", "seq"), P("basis", "seq"))
    return jax.shard_map(
        per_device, mesh=mesh, in_specs=placed, out_specs=P("seq", "basis"), check_vma=False
    )
```

```python
import functools

import jax
import jax.numpy as jnp
from jax import lax
from jax.experimental import pallas as pl
from jax.experimental.pallas import tpu as pltpu
from jax.sharding import PartitionSpec as P

NX, NZ, NC, NL, NY = 4, 4, 2, 2, 4
VMEM = 16 << 20
BIAS = 14.0
PAD = 16


def seq_perm(value, move):
    pairs = []
    for i in range(NX * NZ * NC):
        x, zh, c = move(i // (NZ * NC), i // NC % NZ, i % NC)
        pairs.append((i, ((x % NX) * NZ + zh % NZ) * NC + c % NC))
    return lax.ppermute(value, "seq", pairs)


def basis_perm(value, move):
    pairs = []
    for j in range(NL * NY):
        zl, y = move(j // NY, j % NY)
        pairs.append((j, (zl % NL) * NY + y % NY))
    return lax.ppermute(value, "basis", pairs)


def swap_core(value):
    return seq_perm(value, lambda x, zh, c: (x, zh, c + 1))


def from_x(value, d):
    return seq_perm(value, lambda x, zh, c: (x - d, zh, c))


def from_zh(value, d):
    return seq_perm(value, lambda x, zh, c: (x, zh - d, c))


def from_y(value, d):
    return basis_perm(value, lambda zl, y: (zl, y - d))


def swap_zl(value):
    return basis_perm(value, lambda zl, y: (zl + 1, y))


def to_owner(value, k):
    pairs = []
    for i in range(NX * NZ * NC):
        for j in range(NL * NY):
            xt, zt, c, zl, y = i // (NZ * NC), i // NC % NZ, i % NC, j // NY, j % NY
            x, zh, ahead = xt - xt % 2 + y // 2, 2 * (y % 2) + c, 2 * ((xt % 2) ^ (y // 2)) + (zt + k) % 2
            seq, basis = (x * NZ + zh) * NC + zt // 2, zl * NY + (y + ahead) % NY
            pairs.append((i * NL * NY + j, seq * NL * NY + basis))
    return lax.ppermute(value, ("seq", "basis"), pairs)


def power_of(top):
    return jnp.clip(jnp.ceil(jnp.log2(top)), -100.0, 130.0)


def grow(sent):
    wide = sent.astype(jnp.float32)
    return wide[:-PAD] * jnp.exp2(wide[-PAD : 1 - PAD] - BIAS)


def product_kernel(seq_len, turn, places, left0, left1, left2, *rest):
    grads, (out, left, right, left_sem, right_sem) = rest[:NY], rest[NY:]
    rows = left1.shape[0]
    width = grads[0].shape[1]
    seqs = left.shape[1] // seq_len
    lefts = [
        pltpu.make_async_copy(ref, left.at[pl.ds(at * rows, ref.shape[0]), :], left_sem.at[i])
        for i, (at, ref) in enumerate(((0, left0), (2, left1), (3, left2)))
    ]
    rights = [pltpu.make_async_copy(ref, right.at[g], right_sem.at[g]) for g, ref in enumerate(grads)]
    for copy in lefts + rights:
        copy.start()
    for copy in lefts:
        copy.wait()

    top = jnp.zeros((8, width), jnp.float32)
    for g in range(NY):
        rights[g].wait()

        for m in range(4):
            total = None
            for s in range(seqs):
                from_token = (s + turn) % seqs * seq_len
                product = jnp.dot(
                    left[m * rows : (m + 1) * rows, s * seq_len : (s + 1) * seq_len],
                    right[g, from_token : from_token + seq_len, :],
                    preferred_element_type=jnp.float32,
                )
                total = product * product if total is None else total + product * product
            row = (g % 2 * 2 + m % 2) * rows
            out[places[m // 2 * 2 + g // 2], row : row + rows, :] = total
            top = jnp.maximum(top, jnp.max(total.reshape(rows // 8, 8, width), axis=0))
    power = power_of(jnp.max(jnp.max(top, axis=0, keepdims=True), axis=1, keepdims=True))
    for d in range(NX):
        out[d, : NY * rows, :] = out[d, : NY * rows, :] * jnp.exp2(BIAS - power)
        out[d, NY * rows :, :] = jnp.broadcast_to(power, (PAD, width))


def products(places, left, grads, seq_len, turn):
    half, tokens = left[0].shape
    width = grads[0].shape[1]
    return pl.pallas_call(
        functools.partial(product_kernel, seq_len, turn),
        out_shape=jax.ShapeDtypeStruct((NX, 2 * half + PAD, width), jnp.float32),
        in_specs=[pl.BlockSpec(memory_space=pltpu.SMEM)] + [pl.BlockSpec(memory_space=pl.ANY)] * 7,
        out_specs=pl.BlockSpec(memory_space=pltpu.VMEM),
        scratch_shapes=[
            pltpu.VMEM((2 * half, tokens), jnp.bfloat16),
            pltpu.VMEM((NY, tokens, width), jnp.bfloat16),
            pltpu.SemaphoreType.DMA((3,)),
            pltpu.SemaphoreType.DMA((NY,)),
        ],
        compiler_params=pltpu.CompilerParams(vmem_limit_bytes=VMEM),
        cost_estimate=pl.CostEstimate(
            flops=16 * half * tokens * width, bytes_accessed=10 * tokens * width, transcendentals=0
        ),
    )(places, *left, *grads)


def settle_kernel(value, out, sem):
    copy = pltpu.make_async_copy(value, out, sem)
    copy.start()
    copy.wait()


def settle(value):
    return pl.pallas_call(
        settle_kernel,
        out_shape=jax.ShapeDtypeStruct(value.shape, value.dtype),
        in_specs=[pl.BlockSpec(memory_space=pl.ANY)],
        out_specs=pl.BlockSpec(memory_space=pltpu.VMEM),
        scratch_shapes=[pltpu.SemaphoreType.DMA],
        compiler_params=pltpu.CompilerParams(vmem_limit_bytes=VMEM),
    )(value)


def in_order(pieces, zh):
    twice = jnp.stack(pieces + pieces)
    column = lax.dynamic_slice_in_dim(twice, (NZ - zh) % NZ, NZ, 0)
    return column.reshape(-1, column.shape[2])


def per_device(activations, gradients, act_basis, grad_basis):
    seq_count, seq_len, width = activations.shape
    seq, basis = lax.axis_index("seq"), lax.axis_index("basis")
    x, zh, core = seq // (NZ * NC), seq // NC % NZ, seq % NC
    zl, y = basis // NY, basis % NY
    act = activations.reshape(seq_count * seq_len, width)
    grad = gradients.reshape(seq_count * seq_len, width)

    half = act_basis.shape[0] // 2

    def rows_at(which):
        start = which * half
        return [lax.dynamic_slice_in_dim(shard, start, half, 0).T for shard in (grad_basis, act_basis)]

    kept = jnp.stack(rows_at(core))
    got = swap_core(jnp.stack(rows_at(1 - core)))
    pair = jnp.where(core == 0, jnp.concatenate([kept, got], 1), jnp.concatenate([got, kept], 1))
    pair, grad, act = lax.optimization_barrier((pair, grad, act))
    pieces = [pair] + [from_zh(pair, d) for d in range(1, NZ)]
    grad_sib, act_sib = settle(swap_core(grad)), settle(swap_core(act))
    pieces, grad_sib, act_sib = lax.optimization_barrier((pieces, grad_sib, act_sib))
    grad_column = in_order([piece[0] for piece in pieces], zh)
    act_column = in_order([piece[1] for piece in pieces], zh)
    grad_columns = [grad_column] + [from_x(grad_column, d) for d in range(1, NX)]
    depth = grad_column.shape[0]

    def term(block, columns, d, dims):
        part = lax.dynamic_slice_in_dim(block, (x + d) % NX * depth, depth, 1)
        sides = (part, columns[d]) if dims[0] == 1 else (columns[d], part)
        return lax.dot_general(*sides, ((dims[:1], dims[1:]), ((), ())), preferred_element_type=jnp.float32)

    def begin(blocks, columns, dims):
        sums = [term(block, columns, 0, dims) for block in blocks]
        later, sums = lax.optimization_barrier((columns[2:], sums))
        columns = columns[:2] + later
        return [
            total + term(block, columns, 3, dims) + term(block, columns, 2, dims)
            for block, total in zip(blocks, sums)
        ]

    def end(blocks, columns, dims, sums):
        totals = [total + term(block, columns, 1, dims) for block, total in zip(blocks, sums)]
        return jnp.concatenate([total.astype(jnp.bfloat16) for total in totals], dims[1])

    blocks = [grad, grad_sib]
    sums = begin(blocks, grad_columns, (1, 0))
    grad_columns, act_column, act_sib, sums = lax.optimization_barrier(
        (grad_columns, act_column, act_sib, sums)
    )
    act_columns = [act_column] + [from_x(act_column, d) for d in range(1, NX)]
    rotated_grad = end(blocks, grad_columns, (1, 0), sums)
    blocks = [act, act_sib]
    sums = begin(blocks, act_columns, (0, 1))
    act_columns, fenced, sums = lax.optimization_barrier((act_columns, rotated_grad, sums))
    rotated_act = end(blocks, act_columns, (0, 1), sums)

    far = [from_y(rotated_grad, d) for d in range(1, NY)]
    pieces = [swap_zl(rotated_act[: half // 2]), swap_zl(rotated_act[half // 2 :])]
    far, near, pieces = lax.optimization_barrier((far, rotated_act, pieces))
    mine = [fenced] + far
    other = [swap_core(block) for block in mine]

    number = jnp.arange(NX)
    target = 2 * ((number // 2) ^ zl) + ((number % 2) ^ (y // 2))
    places = ((target - x) % NX).astype(jnp.int32)
    left = [near] + pieces
    terms = [
        products(places, left, mine, seq_len, 0),
        products(places, left, other, seq_len, seq_count),
    ]
    received = [[from_x(term[d].astype(jnp.float16), -d) for d in range(1, NX)] for term in terms]
    received = lax.optimization_barrier(received)
    halves, tops = [], []
    for kept, parts in zip(terms, received):
        half, top = grow(kept[0]), kept[0, -PAD : 1 - PAD]
        for part in parts:
            half = half + grow(part)
            top = jnp.maximum(top, part[-PAD : 1 - PAD].astype(jnp.float32))
        halves.append(half)
        tops.append(top + 2.0)
    total = jnp.where(core == 0, jnp.concatenate(halves, 1), jnp.concatenate(halves[::-1], 1))
    power = jnp.where(core == 0, jnp.concatenate(tops, 1), jnp.concatenate(tops[::-1], 1))
    rows = total.shape[0] // 2
    both = None
    for k in range(2):
        block = lax.dynamic_slice_in_dim(total, (zh + k) % 2 * rows, rows, 0) * jnp.exp2(BIAS - power)
        sent = jnp.concatenate([block, jnp.broadcast_to(power, (PAD, block.shape[1]))]).astype(jnp.float16)
        part = grow(to_owner(sent, k))
        both = part if both is None else both + part
    rows = rows // 2
    final = lax.dynamic_slice_in_dim(both, core * rows, rows, 0)
    final = final + swap_core(lax.dynamic_slice_in_dim(both, (1 - core) * rows, rows, 0))
    all_seqs = seq_count * NX * NZ * NC
    return final / jnp.float32(all_seqs * seq_len)


def solution(mesh):
    placed = (P("seq", None, None), P("seq", None, None), P("basis", "seq"), P("basis", "seq"))
    return jax.shard_map(
        per_device, mesh=mesh, in_specs=placed, out_specs=P("seq", "basis"), check_vma=False
    )
```

```python
import functools

import jax
import jax.numpy as jnp
from jax import lax
from jax.experimental import pallas as pl
from jax.experimental.pallas import tpu as pltpu
from jax.sharding import PartitionSpec as P

NX, NZ, NC, NL, NY = 4, 4, 2, 2, 4
VMEM = 16 << 20
BIAS = 14.0
PAD = 16


def seq_perm(value, move):
    pairs = []
    for i in range(NX * NZ * NC):
        x, zh, c = move(i // (NZ * NC), i // NC % NZ, i % NC)
        pairs.append((i, ((x % NX) * NZ + zh % NZ) * NC + c % NC))
    return lax.ppermute(value, "seq", pairs)


def basis_perm(value, move):
    pairs = []
    for j in range(NL * NY):
        zl, y = move(j // NY, j % NY)
        pairs.append((j, (zl % NL) * NY + y % NY))
    return lax.ppermute(value, "basis", pairs)


def swap_core(value):
    return seq_perm(value, lambda x, zh, c: (x, zh, c + 1))


def from_x(value, d):
    return seq_perm(value, lambda x, zh, c: (x - d, zh, c))


def from_zh(value, d):
    return seq_perm(value, lambda x, zh, c: (x, zh - d, c))


def from_y(value, d):
    return basis_perm(value, lambda zl, y: (zl, y - d))


def swap_zl(value):
    return basis_perm(value, lambda zl, y: (zl + 1, y))


def to_owner(value, k):
    pairs = []
    for i in range(NX * NZ * NC):
        for j in range(NL * NY):
            xt, zt, c, zl, y = i // (NZ * NC), i // NC % NZ, i % NC, j // NY, j % NY
            x, zh, ahead = xt - xt % 2 + y // 2, 2 * (y % 2) + c, 2 * ((xt % 2) ^ (y // 2)) + (zt + k) % 2
            seq, basis = (x * NZ + zh) * NC + zt // 2, zl * NY + (y + ahead) % NY
            pairs.append((i * NL * NY + j, seq * NL * NY + basis))
    return lax.ppermute(value, ("seq", "basis"), pairs)


def power_of(top):
    return jnp.clip(jnp.ceil(jnp.log2(top)), -100.0, 130.0)


def grow(sent):
    wide = sent.astype(jnp.float32)
    return wide[:-PAD] * jnp.exp2(wide[-PAD : 1 - PAD] - BIAS)


def product_kernel(seq_len, turn, places, left0, left1, left2, *rest):
    grads, (out, left, right, left_sem, right_sem) = rest[:NY], rest[NY:]
    rows = left1.shape[0]
    width = grads[0].shape[1]
    seqs = left.shape[1] // seq_len
    lefts = [
        pltpu.make_async_copy(ref, left.at[pl.ds(at * rows, ref.shape[0]), :], left_sem.at[i])
        for i, (at, ref) in enumerate(((0, left0), (2, left1), (3, left2)))
    ]
    rights = [pltpu.make_async_copy(ref, right.at[g], right_sem.at[g]) for g, ref in enumerate(grads)]
    for copy in [lefts[0], rights[0]] + lefts[1:] + rights[1:]:
        copy.start()

    top = jnp.zeros((8, width), jnp.float32)
    for g in range(NY):
        rights[g].wait()

        for m in range(4):
            if g == 0 and m != 1:
                lefts[max(m - 1, 0)].wait()
            total = None
            for s in range(seqs):
                from_token = (s + turn) % seqs * seq_len
                product = jnp.dot(
                    left[m * rows : (m + 1) * rows, s * seq_len : (s + 1) * seq_len],
                    right[g, from_token : from_token + seq_len, :],
                    preferred_element_type=jnp.float32,
                )
                total = product * product if total is None else total + product * product
            row = (g % 2 * 2 + m % 2) * rows
            out[places[m // 2 * 2 + g // 2], row : row + rows, :] = total
            top = jnp.maximum(top, jnp.max(total.reshape(rows // 8, 8, width), axis=0))
    power = power_of(jnp.max(jnp.max(top, axis=0, keepdims=True), axis=1, keepdims=True))
    for d in range(NX):
        out[d, : NY * rows, :] = out[d, : NY * rows, :] * jnp.exp2(BIAS - power)
        out[d, NY * rows :, :] = jnp.broadcast_to(power, (PAD, width))


def products(places, left, grads, seq_len, turn):
    half, tokens = left[0].shape
    width = grads[0].shape[1]
    return pl.pallas_call(
        functools.partial(product_kernel, seq_len, turn),
        out_shape=jax.ShapeDtypeStruct((NX, 2 * half + PAD, width), jnp.float32),
        in_specs=[pl.BlockSpec(memory_space=pltpu.SMEM)] + [pl.BlockSpec(memory_space=pl.ANY)] * 7,
        out_specs=pl.BlockSpec(memory_space=pltpu.VMEM),
        scratch_shapes=[
            pltpu.VMEM((2 * half, tokens), jnp.bfloat16),
            pltpu.VMEM((NY, tokens, width), jnp.bfloat16),
            pltpu.SemaphoreType.DMA((3,)),
            pltpu.SemaphoreType.DMA((NY,)),
        ],
        compiler_params=pltpu.CompilerParams(vmem_limit_bytes=VMEM),
        cost_estimate=pl.CostEstimate(
            flops=16 * half * tokens * width, bytes_accessed=10 * tokens * width, transcendentals=0
        ),
    )(places, *left, *grads)


def settle_kernel(value, out, sem):
    copy = pltpu.make_async_copy(value, out, sem)
    copy.start()
    copy.wait()


def settle(value):
    return pl.pallas_call(
        settle_kernel,
        out_shape=jax.ShapeDtypeStruct(value.shape, value.dtype),
        in_specs=[pl.BlockSpec(memory_space=pl.ANY)],
        out_specs=pl.BlockSpec(memory_space=pltpu.VMEM),
        scratch_shapes=[pltpu.SemaphoreType.DMA],
        compiler_params=pltpu.CompilerParams(vmem_limit_bytes=VMEM),
    )(value)


def in_order(pieces, zh):
    twice = jnp.stack(pieces + pieces)
    column = lax.dynamic_slice_in_dim(twice, (NZ - zh) % NZ, NZ, 0)
    return column.reshape(-1, column.shape[2])


def per_device(activations, gradients, act_basis, grad_basis):
    seq_count, seq_len, width = activations.shape
    seq, basis = lax.axis_index("seq"), lax.axis_index("basis")
    x, zh, core = seq // (NZ * NC), seq // NC % NZ, seq % NC
    zl, y = basis // NY, basis % NY
    act = activations.reshape(seq_count * seq_len, width)
    grad = gradients.reshape(seq_count * seq_len, width)

    half = act_basis.shape[0] // 2

    def rows_at(which):
        start = which * half
        return [lax.dynamic_slice_in_dim(shard, start, half, 0).T for shard in (grad_basis, act_basis)]

    kept = jnp.stack(rows_at(core))
    got = swap_core(jnp.stack(rows_at(1 - core)))
    pair = jnp.where(core == 0, jnp.concatenate([kept, got], 1), jnp.concatenate([got, kept], 1))
    pair, grad, act = lax.optimization_barrier((pair, grad, act))
    pieces = [pair] + [from_zh(pair, d) for d in range(1, NZ)]
    grad_sib, act_sib = settle(swap_core(grad)), settle(swap_core(act))
    pieces, grad_sib, act_sib = lax.optimization_barrier((pieces, grad_sib, act_sib))
    grad_column = in_order([piece[0] for piece in pieces], zh)
    act_column = in_order([piece[1] for piece in pieces], zh)
    grad_columns = [grad_column] + [from_x(grad_column, d) for d in range(1, NX)]
    depth = grad_column.shape[0]

    def term(block, columns, d, dims):
        part = lax.dynamic_slice_in_dim(block, (x + d) % NX * depth, depth, 1)
        sides = (part, columns[d]) if dims[0] == 1 else (columns[d], part)
        return lax.dot_general(*sides, ((dims[:1], dims[1:]), ((), ())), preferred_element_type=jnp.float32)

    def begin(blocks, columns, dims):
        sums = [term(block, columns, 0, dims) for block in blocks]
        later, sums = lax.optimization_barrier((columns[2:], sums))
        columns = columns[:2] + later
        return [
            total + term(block, columns, 3, dims) + term(block, columns, 2, dims)
            for block, total in zip(blocks, sums)
        ]

    def end(blocks, columns, dims, sums):
        totals = [total + term(block, columns, 1, dims) for block, total in zip(blocks, sums)]
        return jnp.concatenate([total.astype(jnp.bfloat16) for total in totals], dims[1])

    blocks = [grad, grad_sib]
    sums = begin(blocks, grad_columns, (1, 0))
    grad_columns, act_column, act_sib, sums = lax.optimization_barrier(
        (grad_columns, act_column, act_sib, sums)
    )
    act_columns = [act_column] + [from_x(act_column, d) for d in range(1, NX)]
    rotated_grad = end(blocks, grad_columns, (1, 0), sums)
    blocks = [act, act_sib]
    sums = begin(blocks, act_columns, (0, 1))
    act_columns, fenced, sums = lax.optimization_barrier((act_columns, rotated_grad, sums))
    rotated_act = end(blocks, act_columns, (0, 1), sums)

    far = [from_y(rotated_grad, d) for d in range(1, NY)]
    pieces = [swap_zl(rotated_act[: half // 2]), swap_zl(rotated_act[half // 2 :])]
    far, near, pieces = lax.optimization_barrier((far, rotated_act, pieces))
    mine = [fenced] + far
    other = [swap_core(block) for block in mine]

    number = jnp.arange(NX)
    target = 2 * ((number // 2) ^ zl) + ((number % 2) ^ (y // 2))
    places = ((target - x) % NX).astype(jnp.int32)
    left = [near] + pieces
    terms = [
        products(places, left, mine, seq_len, 0),
        products(places, left, other, seq_len, seq_count),
    ]
    received = [[from_x(term[d].astype(jnp.float16), -d) for d in range(1, NX)] for term in terms]
    received = lax.optimization_barrier(received)
    halves, tops = [], []
    for kept, parts in zip(terms, received):
        half, top = grow(kept[0]), kept[0, -PAD : 1 - PAD]
        for part in parts:
            half = half + grow(part)
            top = jnp.maximum(top, part[-PAD : 1 - PAD].astype(jnp.float32))
        halves.append(half)
        tops.append(top + 2.0)
    total = jnp.where(core == 0, jnp.concatenate(halves, 1), jnp.concatenate(halves[::-1], 1))
    power = jnp.where(core == 0, jnp.concatenate(tops, 1), jnp.concatenate(tops[::-1], 1))
    rows = total.shape[0] // 2
    both = None
    for k in range(2):
        block = lax.dynamic_slice_in_dim(total, (zh + k) % 2 * rows, rows, 0) * jnp.exp2(BIAS - power)
        sent = jnp.concatenate([block, jnp.broadcast_to(power, (PAD, block.shape[1]))]).astype(jnp.float16)
        part = grow(to_owner(sent, k))
        both = part if both is None else both + part
    rows = rows // 2
    final = lax.dynamic_slice_in_dim(both, core * rows, rows, 0)
    final = final + swap_core(lax.dynamic_slice_in_dim(both, (1 - core) * rows, rows, 0))
    all_seqs = seq_count * NX * NZ * NC
    return final / jnp.float32(all_seqs * seq_len)


def solution(mesh):
    placed = (P("seq", None, None), P("seq", None, None), P("basis", "seq"), P("basis", "seq"))
    return jax.shard_map(
        per_device, mesh=mesh, in_specs=placed, out_specs=P("seq", "basis"), check_vma=False
    )
```
